128 devices in a mesh: mem: 8 (over y, x_lo), seq: 16 (over z, x_hi, core).
Axes of the slice: x: 4 (x_hi: 2, x_lo: 2; x = x_hi * 2 + x_lo), y: 4, z: 4, core: 2. Of those that a mesh axis runs over, the one named last changes fastest.
Arguments:
- state_field: bfloat16 [64, 2048, 512], P('mem', 'seq'), may hold values from -6 to 6
- gain_space: float32 [512], replicated, may hold values from 0.25 to 1.75
- w_qkv_space: bfloat16 [512, 1536], replicated, may hold values from -0.2788369 to 0.2788369
- w_out_space: bfloat16 [512, 512], replicated, may hold values from -0.25 to 0.25
- gain_member: float32 [512], replicated, may hold values from 0.25 to 1.75
- w_qkv_member: bfloat16 [512, 1536], replicated, may hold values from -0.28079004 to 0.28079004
- w_out_member: bfloat16 [512, 512], replicated, may hold values from -0.25 to 0.25
- gain_mlp: float32 [512], replicated, may hold values from 0.25 to 1.75
- w_up: bfloat16 [512, 2048], replicated, may hold values from -0.25 to 0.25
- w_down: bfloat16 [2048, 512], replicated, may hold values from -0.125 to 0.125
Outputs:
- corrected: bfloat16 [64, 2048, 512], P('mem', 'seq')
The draws below stay inside these ranges and needn't reach their ends.
All inputs are finite; a program needn't handle non-finite values.
Results may differ from the reference program's by a relative error of at most 0.018.
Values may be sent and summed in bfloat16 or wider, within the bound.
No kernel may reach another device: no remote copies, remote signals or barrier semaphores. Data moves between devices by JAX's collectives and lax.ppermute only.
A program may use at most 256 MiB of HBM per device.

```python
import jax
import jax.numpy as jnp
from jax import lax

D = 512
HEADS = 8
FF = 2048
MEMBERS = 64
TOKENS = 2048


def drawn_weight(key):
    base_weight = jax.random.truncated_normal(key, -6.0, 6.0, (D, 3 * D), jnp.float32) * D ** (-0.5)
    return base_weight


def draw_state_field(key, part):
    key = jax.random.fold_in(key, 1)
    base_noise = jax.random.truncated_normal(key, -6.0, 6.0, (MEMBERS, TOKENS, D), jnp.float32)
    return base_noise.astype(jnp.bfloat16)


def draw_w_qkv_space(key, part):
    key = jax.random.fold_in(key, 5)
    return drawn_weight(key).astype(jnp.bfloat16)


def draw_w_qkv_member(key, part):
    key = jax.random.fold_in(key, 7)
    return drawn_weight(key).astype(jnp.bfloat16)


def gaussian(stream_key, dims, deviation, limit, kind=jnp.bfloat16):
    return jnp.clip(deviation * jax.random.normal(stream_key, dims, jnp.float32), -limit, limit).astype(kind)


def setup_inputs(seed: int = 0) -> dict:
    streams_of = jax.random.split(jax.random.key(seed), 11)
    state_field = draw_state_field(jax.random.fold_in(streams_of[10], 71), 0)
    gain_space = jnp.clip(1.0 + 0.15 * jax.random.normal(streams_of[1], (D,), jnp.float32), 0.25, 1.75)
    w_qkv_space = draw_w_qkv_space(jax.random.fold_in(streams_of[10], 71), 0)
    w_out_space = gaussian(streams_of[3], (D, D), D ** -0.5, 0.25)
    gain_member = jnp.clip(1.0 + 0.15 * jax.random.normal(streams_of[4], (D,), jnp.float32), 0.25, 1.75)
    w_qkv_member = draw_w_qkv_member(jax.random.fold_in(streams_of[10], 71), 0)
    w_out_member = gaussian(streams_of[6], (D, D), D ** -0.5, 0.25)
    gain_mlp = jnp.clip(1.0 + 0.15 * jax.random.normal(streams_of[7], (D,), jnp.float32), 0.25, 1.75)
    w_up = gaussian(streams_of[8], (D, FF), D ** -0.5, 0.25)
    w_down = gaussian(streams_of[9], (FF, D), FF ** -0.5, 0.125)
    return dict(state_field=state_field, gain_space=gain_space, w_qkv_space=w_qkv_space, w_out_space=w_out_space, gain_member=gain_member, w_qkv_member=w_qkv_member, w_out_member=w_out_member, gain_mlp=gain_mlp, w_up=w_up, w_down=w_down)


def normed(values, gain):
    floats = values.astype(jnp.float32)
    scaled = floats * lax.rsqrt(lax.optimization_barrier(jnp.mean(floats * floats, axis=-1, keepdims=True)) + 1e-05)
    return (scaled * gain).astype(jnp.bfloat16)

def space_single(member_qkv):
    head_dim = D // HEADS
    shaped = member_qkv.reshape(member_qkv.shape[0], 3, HEADS, head_dim).astype(jnp.float32)
    scores = jnp.einsum('qhc,khc->hqk', shaped[:, 0], shaped[:, 1]) * head_dim ** (-0.5)
    peaks = lax.optimization_barrier(jnp.max(scores, axis=-1, keepdims=True))
    weights = jnp.exp(scores - peaks)
    totals = lax.optimization_barrier(jnp.sum(weights, axis=-1))
    rounded = weights.astype(jnp.bfloat16).astype(jnp.float32)
    mixed = jnp.einsum('hqk,khc->qhc', rounded, shaped[:, 2]) / jnp.transpose(totals)[:, :, None]
    return mixed.reshape(member_qkv.shape[0], D).astype(jnp.bfloat16)

def member_attend(queries, key_value):
    head_dim = D // HEADS
    count, tokens_here = (queries.shape[0], queries.shape[1])
    q = queries.reshape(count, tokens_here, HEADS, head_dim).astype(jnp.float32)
    k = key_value[..., :D].reshape(key_value.shape[0], tokens_here, HEADS, head_dim).astype(jnp.float32)
    v = key_value[..., D:].reshape(key_value.shape[0], tokens_here, HEADS, head_dim).astype(jnp.float32)
    scores = jnp.einsum('mthc,nthc->thmn', q, k) * head_dim ** (-0.5)
    peaks = lax.optimization_barrier(jnp.max(scores, axis=-1, keepdims=True))
    weights = jnp.exp(scores - peaks)
    totals = lax.optimization_barrier(jnp.sum(weights, axis=-1))
    rounded = weights.astype(jnp.bfloat16).astype(jnp.float32)
    mixed = jnp.einsum('thmn,nthc->mthc', rounded, v) / jnp.transpose(totals, (2, 0, 1))[..., None]
    return mixed.reshape(count, tokens_here, D).astype(jnp.bfloat16)

def project(values, weight):
    rows = values.reshape(-1, values.shape[-1])
    return jnp.dot(rows, weight, preferred_element_type=jnp.float32).reshape(values.shape[:-1] + (weight.shape[1],))

def reference(state_field, gain_space, w_qkv_space, w_out_space, gain_member, w_qkv_member, w_out_member, gain_mlp, w_up, w_down):
    qkv_space = project(normed(state_field, gain_space), w_qkv_space).astype(jnp.bfloat16)
    spatial = lax.map(space_single, qkv_space)
    after_space = (state_field.astype(jnp.float32) + project(spatial, w_out_space)).astype(jnp.bfloat16)
    qkv_member = project(normed(after_space, gain_member), w_qkv_member).astype(jnp.bfloat16)
    member_mix = member_attend(qkv_member[..., :D], qkv_member[..., D:])
    after_member = (after_space.astype(jnp.float32) + project(member_mix, w_out_member)).astype(jnp.bfloat16)
    hidden = jax.nn.gelu(project(normed(after_member, gain_mlp), w_up), approximate=True).astype(jnp.bfloat16)
    return (after_member.astype(jnp.float32) + project(hidden, w_down)).astype(jnp.bfloat16)
```

```python
import functools
import math

import jax
import jax.numpy as jnp
from jax import lax
from jax.experimental import pallas as pl
from jax.experimental.pallas import tpu as pltpu
from jax.sharding import Mesh, PartitionSpec as P

HEADS = 8
LANES = 128
SCORE_SCALE = math.log2(math.e)
VMEM_LIMIT = 48 * 1024 * 1024
NT = (((1,), (1,)), ((), ()))


def params():
    return pltpu.CompilerParams(vmem_limit_bytes=VMEM_LIMIT)


def normed(values, gain):
    scaled = values * lax.rsqrt(jnp.mean(values * values, axis=-1, keepdims=True) + 1e-05)
    return (scaled * gain).astype(jnp.bfloat16)


def dot(a, b):
    return jnp.dot(a, b, preferred_element_type=jnp.float32)


def lane_is_low(shape):
    return lax.broadcasted_iota(jnp.int32, shape, 1) < LANES // 2


def qkv_kernel(x_ref, gain_ref, w_ref, q_ref, k_ref, v_ref):
    width = x_ref.shape[-1]
    scale = (width // HEADS) ** (-0.5) * SCORE_SCALE
    rows = normed(x_ref[...].astype(jnp.float32), gain_ref[...])
    qkv = dot(rows, w_ref[...])
    q_ref[...] = (qkv[:, :width] * scale).astype(jnp.bfloat16)
    k_ref[...] = qkv[:, width : 2 * width].astype(jnp.bfloat16)
    v_ref[...] = qkv[:, 2 * width :].astype(jnp.bfloat16)


def project_qkv(x, gain, w, block=256):
    rows, width = x.shape
    row_spec = pl.BlockSpec((block, width), lambda i: (i, 0))
    return pl.pallas_call(
        qkv_kernel,
        grid=(rows // block,),
        in_specs=[
            row_spec,
            pl.BlockSpec((1, width), lambda i: (0, 0)),
            pl.BlockSpec((width, 3 * width), lambda i: (0, 0)),
        ],
        out_specs=[row_spec] * 3,
        out_shape=[jax.ShapeDtypeStruct((rows, width), jnp.bfloat16)] * 3,
        compiler_params=params(),
        name="space_qkv",
    )(x, gain, w)


def attend_kernel(q_ref, k0_ref, k1_ref, v0_ref, v1_ref, x_ref, w_ref, o_ref, kt, vz, att):
    half, width = k0_ref.shape
    head_dim = width // HEADS

    @pl.when(pl.program_id(0) == 0)
    def _():
        for part, (k_ref, v_ref) in enumerate(((k0_ref, v0_ref), (k1_ref, v1_ref))):
            kt[:, part * half : (part + 1) * half] = k_ref[...].T
            for pair in range(HEADS // 2):
                values = v_ref[:, pair * LANES : (pair + 1) * LANES]
                low = lane_is_low(values.shape)
                one = jnp.ones_like(values)
                vz[2 * pair, part * half : (part + 1) * half, :] = jnp.where(low, values, one)
                vz[2 * pair + 1, part * half : (part + 1) * half, :] = jnp.where(low, one, values)

    rows = q_ref.shape[0]
    low = lane_is_low((rows, LANES))
    for pair in range(HEADS // 2):
        lanes = slice(pair * LANES, (pair + 1) * LANES)
        queries = q_ref[:, lanes]
        none = jnp.zeros_like(queries)
        parts = []
        for odd in range(2):
            mine = jnp.where(low, none, queries) if odd else jnp.where(low, queries, none)
            scores = dot(mine, kt[lanes, :])
            peaks = jnp.max(scores, axis=-1, keepdims=True)
            weights = jnp.exp2(scores - peaks).astype(jnp.bfloat16)
            mixed = dot(weights, vz[2 * pair + odd])
            parts.append(mixed / pltpu.roll(mixed, LANES // 2, 1))
        att[:, lanes] = jnp.where(low, parts[0], parts[1]).astype(jnp.bfloat16)
    o_ref[...] = (x_ref[...].astype(jnp.float32) + dot(att[...], w_ref[...])).astype(jnp.bfloat16)


def attend(q, k0, k1, v0, v1, x, w, block=256):
    rows, width = q.shape
    keys = k0.shape[0]
    row_spec = pl.BlockSpec((block, width), lambda i: (i, 0))
    key_spec = pl.BlockSpec((keys, width), lambda i: (0, 0))
    return pl.pallas_call(
        attend_kernel,
        grid=(rows // block,),
        in_specs=[row_spec] + [key_spec] * 4 + [row_spec, pl.BlockSpec((width, width), lambda i: (0, 0))],
        out_specs=row_spec,
        out_shape=jax.ShapeDtypeStruct((rows, width), jnp.bfloat16),
        scratch_shapes=[
            pltpu.VMEM((width, 2 * keys), jnp.bfloat16),
            pltpu.VMEM((HEADS, 2 * keys, LANES), jnp.bfloat16),
            pltpu.VMEM((block, width), jnp.bfloat16),
        ],
        compiler_params=params(),
        name="space_attend",
    )(q, k0, k1, v0, v1, x, w)


def member_kernel(
    group, x_ref, gain_ref, wqkv_ref, wout_ref, gain2_ref, wup_ref, wdown_ref, o_ref, xf, of, att
):
    members, tokens, width = x_ref.shape
    scale = (width // HEADS) ** (-0.5) * SCORE_SCALE
    step = pl.program_id(0)

    @pl.when(step == 0)
    def _():
        flat = x_ref[...].reshape(members * tokens, width).astype(jnp.float32)
        for c in range(width // LANES):
            xf[c] = flat[:, c * LANES : (c + 1) * LANES]

    rows = group * members
    lines = [
        jnp.concatenate(
            [xf[c, pl.ds(step * group + t, members, stride=tokens), :] for c in range(width // LANES)],
            axis=1,
        )
        for t in range(group)
    ]
    x = jnp.concatenate(lines, axis=0)
    qkv = dot(normed(x, gain_ref[...]), wqkv_ref[...])
    low = lane_is_low((rows, LANES))
    same = (
        lax.broadcasted_iota(jnp.int32, (rows, rows), 0) // members
        == lax.broadcasted_iota(jnp.int32, (rows, rows), 1) // members
    )
    for pair in range(HEADS // 2):
        lo, hi = pair * LANES, (pair + 1) * LANES
        queries = (qkv[:, lo:hi] * scale).astype(jnp.bfloat16)
        keys = qkv[:, width + lo : width + hi].astype(jnp.bfloat16)
        values = qkv[:, 2 * width + lo : 2 * width + hi].astype(jnp.bfloat16)
        none, one = jnp.zeros_like(queries), jnp.ones_like(values)
        parts = []
        for odd in range(2):
            mine = jnp.where(low, none, queries) if odd else jnp.where(low, queries, none)
            scores = lax.dot_general(mine, keys, NT, preferred_element_type=jnp.float32)
            scores = jnp.where(same, scores, -jnp.inf)
            peaks = jnp.max(scores, axis=-1, keepdims=True)
            weights = jnp.exp2(scores - peaks).astype(jnp.bfloat16)
            mixed = dot(weights, jnp.where(low, one, values) if odd else jnp.where(low, values, one))
            parts.append(mixed / pltpu.roll(mixed, LANES // 2, 1))
        att[:, lo:hi] = jnp.where(low, parts[0], parts[1]).astype(jnp.bfloat16)
    after = (x + dot(att[...], wout_ref[...])).astype(jnp.bfloat16).astype(jnp.float32)
    up = dot(normed(after, gain2_ref[...]), wup_ref[...])
    hidden = jax.nn.gelu(up, approximate=True).astype(jnp.bfloat16)
    out = after + dot(hidden, wdown_ref[...])
    for t in range(group):
        for c in range(width // LANES):
            of[c, pl.ds(step * group + t, members, stride=tokens), :] = out[
                t * members : (t + 1) * members, c * LANES : (c + 1) * LANES
            ]

    @pl.when(step == pl.num_programs(0) - 1)
    def _():
        for c in range(width // LANES):
            o_ref[:, :, c * LANES : (c + 1) * LANES] = (
                of[c].astype(jnp.bfloat16).reshape(members, tokens, LANES)
            )


def member_part(x, gain, wqkv, wout, gain2, wup, wdown, group=4):
    members, tokens, width = x.shape
    ff = wup.shape[1]

    def whole(*shape):
        return pl.BlockSpec(shape, lambda i: (0,) * len(shape))

    return pl.pallas_call(
        functools.partial(member_kernel, group),
        grid=(tokens // group,),
        in_specs=[
            whole(members, tokens, width),
            whole(1, width),
            whole(width, 3 * width),
            whole(width, width),
            whole(1, width),
            whole(width, ff),
            whole(ff, width),
        ],
        out_specs=whole(members, tokens, width),
        out_shape=jax.ShapeDtypeStruct((members, tokens, width), jnp.bfloat16),
        scratch_shapes=[
            pltpu.VMEM((width // LANES, members * tokens, LANES), jnp.float32),
            pltpu.VMEM((width // LANES, members * tokens, LANES), jnp.float32),
            pltpu.VMEM((group * members, width), jnp.bfloat16),
        ],
        compiler_params=params(),
        name="member_part",
    )(x, gain, wqkv, wout, gain2, wup, wdown)


def per_device(
    state_field,
    gain_space,
    w_qkv_space,
    w_out_space,
    gain_member,
    w_qkv_member,
    w_out_member,
    gain_mlp,
    w_up,
    w_down,
):
    mem_dev, tok_dev, width = state_field.shape
    n_mem, n_grp = lax.axis_size("mem"), lax.axis_size("grp")
    gain_space, gain_member, gain_mlp = (g[None] for g in (gain_space, gain_member, gain_mlp))
    with jax.named_scope("tokens_to_member"):
        mine = lax.all_to_all(state_field, "grp", split_axis=0, concat_axis=0, tiled=True)
    x = mine.reshape(n_grp * tok_dev, width)
    q, k, v = project_qkv(x, gain_space, w_qkv_space)
    with jax.named_scope("keys_of_other_core"):
        k_other, v_other = (lax.ppermute(a, "core", [(0, 1), (1, 0)]) for a in (k, v))
    after_space = attend(q, k, k_other, v, v_other, x, w_out_space)
    here = tok_dev // n_mem
    sent = after_space.reshape(n_grp * n_mem, here, width)
    with jax.named_scope("members_to_tokens"):
        tokens = lax.all_to_all(sent, ("grp", "mem"), split_axis=0, concat_axis=0, tiled=True)
    out = member_part(
        tokens, gain_member, w_qkv_member, w_out_member, gain_mlp, w_up, w_down
    )
    out = out.reshape(n_grp, n_mem, here, width).transpose(1, 0, 2, 3)
    with jax.named_scope("tokens_back"):
        back = lax.all_to_all(out, "mem", split_axis=0, concat_axis=0, tiled=True)
    return back.transpose(1, 0, 2, 3).reshape(mem_dev, tok_dev, width)


def solution(mesh):
    grid = Mesh(mesh.devices.reshape(8, 8, 2), ("mem", "grp", "core"))
    rows = P("mem", ("grp", "core"), None)
    return jax.shard_map(
        per_device, mesh=grid, in_specs=(rows,) + (P(),) * 9, out_specs=rows, check_vma=False
    )
```

```python
import functools
import math

import jax
import jax.numpy as jnp
from jax import lax
from jax.experimental import pallas as pl
from jax.experimental.pallas import tpu as pltpu
from jax.sharding import Mesh, PartitionSpec as P

HEADS = 8
LANES = 128
SCORE_SCALE = math.log2(math.e)
VMEM_LIMIT = 24 * 1024 * 1024
NT = (((1,), (1,)), ((), ()))


def params():
    return pltpu.CompilerParams(vmem_limit_bytes=VMEM_LIMIT)


def cost(flops, moved):
    return pl.CostEstimate(flops=int(flops), bytes_accessed=int(moved), transcendentals=0)


def normed(values, gain):
    scaled = values * lax.rsqrt(jnp.mean(values * values, axis=-1, keepdims=True) + 1e-05)
    return (scaled * gain).astype(jnp.bfloat16)


def dot(a, b):
    return jnp.dot(a, b, preferred_element_type=jnp.float32)


def lane_is_low(shape):
    return lax.broadcasted_iota(jnp.int32, shape, 1) < LANES // 2


def qkv_kernel(want_q, x_ref, gain_ref, w_ref, *outs):
    width = x_ref.shape[-1]
    scale = (width // HEADS) ** (-0.5) * SCORE_SCALE
    q_ref, kt_ref, vz_ref = outs if want_q else (None,) + outs
    rows = normed(x_ref[...].astype(jnp.float32), gain_ref[...])
    if want_q:
        q_ref[...] = (dot(rows, w_ref[:, :width]) * scale).astype(jnp.bfloat16)
    kt_ref[...] = dot(rows, w_ref[:, width : 2 * width]).astype(jnp.bfloat16).T
    values = dot(rows, w_ref[:, 2 * width :]).astype(jnp.bfloat16)
    for pair in range(HEADS // 2):
        mine = values[:, pair * LANES : (pair + 1) * LANES]
        low = lane_is_low(mine.shape)
        one = jnp.ones_like(mine)
        vz_ref[2 * pair] = jnp.where(low, mine, one)
        vz_ref[2 * pair + 1] = jnp.where(low, one, mine)


def project_qkv(x, gain, w, want_q, block=256):
    rows, width = x.shape
    row_spec = pl.BlockSpec((block, width), lambda i: (i, 0))
    out_specs = [
        row_spec,
        pl.BlockSpec((width, block), lambda i: (0, i)),
        pl.BlockSpec((HEADS, block, LANES), lambda i: (0, i, 0)),
    ]
    out_shape = [
        jax.ShapeDtypeStruct((rows, width), jnp.bfloat16),
        jax.ShapeDtypeStruct((width, rows), jnp.bfloat16),
        jax.ShapeDtypeStruct((HEADS, rows, LANES), jnp.bfloat16),
    ]
    return pl.pallas_call(
        functools.partial(qkv_kernel, want_q),
        grid=(rows // block,),
        in_specs=[
            row_spec,
            pl.BlockSpec((1, width), lambda i: (0, 0)),
            pl.BlockSpec((width, 3 * width), lambda i: (0, 0)),
        ],
        out_specs=out_specs if want_q else out_specs[1:],
        out_shape=out_shape if want_q else out_shape[1:],
        compiler_params=params(),
        cost_estimate=cost(2 * rows * width * width * (3 if want_q else 2), 6 * rows * width),
        name="space_qkv" if want_q else "space_kv",
    )(x, gain, w)


def attend_kernel(block, keys_step, q_ref, kt0, kt1, vz0, vz1, x_ref, w_ref, o_ref, held, att):
    rows = q_ref.shape[0]
    half = kt0.shape[1]
    steps = 2 * half // keys_step
    blocks = rows // block
    low = lane_is_low((block, LANES))

    def place(step):
        at = step % (steps // 2) * keys_step
        return step >= steps // 2, slice(at, at + keys_step)

    def head_queries(at, head):
        pair = head // 2
        queries = q_ref[pl.ds(at * block, block), pair * LANES : (pair + 1) * LANES]
        none = jnp.zeros_like(queries)
        return jnp.where(low, none, queries) if head % 2 else jnp.where(low, queries, none)

    def score(queries, head, step, slot, peak):
        second, cols = place(step)
        pair = head // 2
        keys = (kt1 if second else kt0)[pair * LANES : (pair + 1) * LANES, cols]
        scores = dot(queries, keys)
        held[slot, :, step * keys_step : (step + 1) * keys_step] = scores
        for c in range(keys_step // LANES):
            part = scores[:, c * LANES : (c + 1) * LANES]
            peak = part if peak is None else jnp.maximum(peak, part)
        return peak

    def mix(head, step, slot, peaks):
        second, cols = place(step)
        scores = held[slot, :, step * keys_step : (step + 1) * keys_step]
        weights = jnp.exp2(scores - peaks).astype(jnp.bfloat16)
        return dot(weights, (vz1 if second else vz0)[head, cols, :])

    def row_peaks(peak):
        return jnp.max(peak, axis=-1, keepdims=True)

    peak = None
    first = head_queries(0, 0)
    for step in range(steps):
        peak = score(first, 0, step, 0, peak)

    def body(at, peaks):
        even = None
        for head in range(HEADS):
            after = (head + 1) % HEADS
            queries = head_queries(at if after else jnp.minimum(at + 1, blocks - 1), after)
            peak, mixed = None, None
            for step in range(steps):
                part = mix(head, step, head % 2, peaks)
                mixed = part if mixed is None else mixed + part
                peak = score(queries, after, step, after % 2, peak)
            peaks = row_peaks(peak)
            mixed = mixed / pltpu.roll(mixed, LANES // 2, 1)
            if head % 2:
                pair = head // 2
                att[:, pair * LANES : (pair + 1) * LANES] = jnp.where(low, even, mixed).astype(
                    jnp.bfloat16
                )
            even = mixed
        here = pl.ds(at * block, block)
        out = x_ref[here, :].astype(jnp.float32) + dot(att[...], w_ref[...])
        o_ref[here, :] = out.astype(jnp.bfloat16)
        return peaks

    lax.fori_loop(0, blocks, body, row_peaks(peak))


def attend(q, kt0, kt1, vz0, vz1, x, w, block=512, keys_step=256):
    rows, width = q.shape
    keys = 2 * kt0.shape[1]
    in_vmem = pl.BlockSpec(memory_space=pltpu.VMEM)
    return pl.pallas_call(
        functools.partial(attend_kernel, block, keys_step),
        in_specs=[in_vmem] * 7,
        out_specs=in_vmem,
        out_shape=jax.ShapeDtypeStruct((rows, width), jnp.bfloat16),
        scratch_shapes=[
            pltpu.VMEM((2, block, keys), jnp.float32),
            pltpu.VMEM((block, width), jnp.bfloat16),
        ],
        compiler_params=params(),
        cost_estimate=cost(16 * rows * keys * width, 12 * keys * width),
        name="space_attend",
    )(q, kt0, kt1, vz0, vz1, x, w)


def member_kernel(
    block, ff_step, ahead, x_ref, gain_ref, wqkv_ref, wout_ref, gain2_ref, wup_ref, wdown_ref,
    o_ref, rows32, qs, ks, vs, att,
):
    members, tokens, width = x_ref.shape
    ff = wup_ref.shape[1]
    total = members * tokens
    scale = (width // HEADS) ** (-0.5) * SCORE_SCALE
    columns = range(width // LANES)
    flat = x_ref[...].reshape(total, width).astype(jnp.float32)
    for c in columns:
        rows32[c] = flat[:, c * LANES : (c + 1) * LANES]

    def lane_slice(c):
        return slice(c * LANES, (c + 1) * LANES)

    def token_rows(token):
        parts = [rows32[c, pl.ds(token, members, stride=tokens), :] for c in columns]
        return jnp.concatenate(parts, axis=1)

    per_block = block // members
    xs = []
    for b in range(total // block):
        here = slice(b * block, (b + 1) * block)
        x = jnp.concatenate([token_rows(b * per_block + t) for t in range(per_block)], axis=0)
        xs.append(x)
        n = normed(x, gain_ref[...])
        qs[here, :] = (dot(n, wqkv_ref[:, :width]) * scale).astype(jnp.bfloat16)
        ks[here, :] = dot(n, wqkv_ref[:, width : 2 * width]).astype(jnp.bfloat16)
        vs[here, :] = dot(n, wqkv_ref[:, 2 * width :]).astype(jnp.bfloat16)

    tile = 4 * members
    low = lane_is_low((tile, LANES))
    same = (
        lax.broadcasted_iota(jnp.int32, (tile, tile), 0) // members
        == lax.broadcasted_iota(jnp.int32, (tile, tile), 1) // members
    )
    work = [
        (slice(g * tile, (g + 1) * tile), lane_slice(h // 2), h % 2)
        for g in range(total // tile)
        for h in range(HEADS)
    ]

    def score(rows, lanes, odd):
        queries = qs[rows, lanes]
        none = jnp.zeros_like(queries)
        queries = jnp.where(low, none, queries) if odd else jnp.where(low, queries, none)
        return lax.dot_general(queries, ks[rows, lanes], NT, preferred_element_type=jnp.float32)

    pending = [score(*w) for w in work[:ahead]]
    even = None
    for i, (rows, lanes, odd) in enumerate(work):
        scores = pending.pop(0)
        if i + ahead < len(work):
            pending.append(score(*work[i + ahead]))
        scores = jnp.where(same, scores, -jnp.inf)
        peaks = jnp.max(scores, axis=-1, keepdims=True)
        weights = jnp.exp2(scores - peaks).astype(jnp.bfloat16)
        values = vs[rows, lanes]
        one = jnp.ones_like(values)
        mixed = dot(weights, jnp.where(low, one, values) if odd else jnp.where(low, values, one))
        mixed = mixed / pltpu.roll(mixed, LANES // 2, 1)
        if odd:
            att[rows, lanes] = jnp.where(low, even, mixed).astype(jnp.bfloat16)
        even = mixed

    for b in range(total // block):
        here = slice(b * block, (b + 1) * block)
        after = (xs[b] + dot(att[here, :], wout_ref[...])).astype(jnp.bfloat16).astype(jnp.float32)
        out = after
        n = normed(after, gain2_ref[...])
        up = dot(n, wup_ref[:, :ff_step])
        for j in range(0, ff, ff_step):
            later = dot(n, wup_ref[:, j + ff_step : j + 2 * ff_step]) if j + ff_step < ff else None
            hidden = jax.nn.gelu(up, approximate=True).astype(jnp.bfloat16)
            out = out + dot(hidden, wdown_ref[j : j + ff_step, :])
            up = later
        for t in range(per_block):
            for c in columns:
                rows32[c, pl.ds(b * per_block + t, members, stride=tokens), :] = out[
                    t * members : (t + 1) * members, lane_slice(c)
                ]
    for c in columns:
        o_ref[:, :, lane_slice(c)] = (
            rows32[c].astype(jnp.bfloat16).reshape(members, tokens, LANES)
        )


def member_part(x, gain, wqkv, wout, gain2, wup, wdown, block=256, ff_step=512, ahead=4):
    members, tokens, width = x.shape
    total, ff = members * tokens, wup.shape[1]
    in_vmem = pl.BlockSpec(memory_space=pltpu.VMEM)
    return pl.pallas_call(
        functools.partial(member_kernel, block, ff_step, ahead),
        in_specs=[in_vmem] * 7,
        out_specs=in_vmem,
        out_shape=jax.ShapeDtypeStruct((members, tokens, width), jnp.bfloat16),
        scratch_shapes=[pltpu.VMEM((width // LANES, total, LANES), jnp.float32)]
        + [pltpu.VMEM((total, width), jnp.bfloat16)] * 4,
        compiler_params=params(),
        cost_estimate=cost(total * width * 2 * (4 * width + 2 * ff) * 2, 6 * total * width),
        name="member_part",
    )(x, gain, wqkv, wout, gain2, wup, wdown)


def per_device(
    state_field,
    gain_space,
    w_qkv_space,
    w_out_space,
    gain_member,
    w_qkv_member,
    w_out_member,
    gain_mlp,
    w_up,
    w_down,
):
    mem_dev, tok_dev, width = state_field.shape
    n_mem, n_grp = lax.axis_size("mem"), lax.axis_size("grp")
    gain_space, gain_member, gain_mlp = (g[None] for g in (gain_space, gain_member, gain_mlp))
    with jax.named_scope("tokens_to_member"):
        mine = lax.all_to_all(state_field, "grp", split_axis=0, concat_axis=0, tiled=True)
    x = mine.reshape(n_grp * tok_dev, width)
    with jax.named_scope("rows_of_other_core"):
        x_other = lax.ppermute(x, "core", [(0, 1), (1, 0)])
    q, kt, vz = project_qkv(x, gain_space, w_qkv_space, True)
    kt_other, vz_other = project_qkv(x_other, gain_space, w_qkv_space, False)
    after_space = attend(q, kt, kt_other, vz, vz_other, x, w_out_space)
    here = tok_dev // n_mem
    sent = after_space.reshape(n_grp * n_mem, here, width)
    with jax.named_scope("members_to_tokens"):
        tokens = lax.all_to_all(sent, ("grp", "mem"), split_axis=0, concat_axis=0, tiled=True)
    out = member_part(tokens, gain_member, w_qkv_member, w_out_member, gain_mlp, w_up, w_down)
    out = out.reshape(n_grp, n_mem, here, width).transpose(1, 0, 2, 3)
    with jax.named_scope("tokens_back"):
        back = lax.all_to_all(out, "mem", split_axis=0, concat_axis=0, tiled=True)
    return back.transpose(1, 0, 2, 3).reshape(mem_dev, tok_dev, width)


def solution(mesh):
    grid = Mesh(mesh.devices.reshape(8, 8, 2), ("mem", "grp", "core"))
    rows = P("mem", ("grp", "core"), None)
    return jax.shard_map(
        per_device, mesh=grid, in_specs=(rows,) + (P(),) * 9, out_specs=rows, check_vma=False
    )
```

```python
import functools
import math

import jax
import jax.numpy as jnp
from jax import lax
from jax.experimental import pallas as pl
from jax.experimental.pallas import tpu as pltpu
from jax.sharding import Mesh, PartitionSpec as P

HEADS = 8
LANES = 128
SCORE_SCALE = math.log2(math.e)
SMALL = jnp.float8_e4m3fn
NT = (((1,), (1,)), ((), ()))


def params(mib):
    return pltpu.CompilerParams(vmem_limit_bytes=mib * 1024 * 1024)


def cost(flops, moved):
    return pl.CostEstimate(flops=int(flops), bytes_accessed=int(moved), transcendentals=0)


def normed(values, gain):
    scaled = values * lax.rsqrt(jnp.mean(values * values, axis=-1, keepdims=True) + 1e-05)
    return (scaled * gain).astype(jnp.bfloat16)


def dot(a, b):
    return jnp.dot(a, b, preferred_element_type=jnp.float32)


def lane_is_low(shape):
    return lax.broadcasted_iota(jnp.int32, shape, 1) < LANES // 2


def high_low(values):
    high = values.astype(SMALL).astype(jnp.bfloat16)
    return high, values - high


def turned(values):
    return jnp.concatenate([values[:, LANES // 2 :], values[:, : LANES // 2]], axis=1)


def put_queries(q_ref, here, q):
    for pair in range(HEADS // 2):
        high, low_part = high_low(q[:, pair * LANES : (pair + 1) * LANES].astype(jnp.bfloat16))
        low_part = low_part * 4
        quarter = high * 0.25
        first = lane_is_low(high.shape)
        even, odd = 2 * pair, 2 * pair + 1
        q_ref[even, here, :LANES] = jnp.where(first, high, turned(quarter)).astype(SMALL)
        q_ref[even, here, LANES:] = jnp.where(first, low_part, turned(low_part)).astype(SMALL)
        q_ref[odd, here, :LANES] = jnp.where(first, turned(high), quarter).astype(SMALL)
        q_ref[odd, here, LANES:] = jnp.where(first, turned(low_part), low_part).astype(SMALL)


def put_keys(kt_ref, here, k):
    high, low = high_low(k.astype(jnp.bfloat16).T)
    parts = [p.astype(SMALL) for p in (high, low * 4, high * 0.25, low * 0.25)]
    dim = high.shape[0] // HEADS
    for head in range(HEADS):
        for i, part in enumerate(parts):
            kt_ref[head, i * dim : (i + 1) * dim, here] = part[head * dim : (head + 1) * dim]


def qkv_kernel(want_q, block, x_ref, gain_ref, w_ref, *outs):
    total, width = x_ref.shape
    q_scale = SCORE_SCALE * 2 * (width // HEADS) ** (-0.5)
    for b in range(total // block):
        here = slice(b * block, (b + 1) * block)
        rows = normed(x_ref[here, :].astype(jnp.float32), gain_ref[...])
        if want_q:
            put_queries(outs[0], here, dot(rows, w_ref[:, :width]) * q_scale)
        put_keys(outs[-2], here, dot(rows, w_ref[:, width : 2 * width]) * 0.5)
        outs[-1][here, :] = dot(rows, w_ref[:, 2 * width :]).astype(jnp.bfloat16)


def project_qkv(x, gain, w, want_q, block=512):
    rows, width = x.shape
    in_vmem = pl.BlockSpec(memory_space=pltpu.VMEM)
    out_shape = [
        jax.ShapeDtypeStruct((HEADS, rows, 2 * LANES), SMALL),
        jax.ShapeDtypeStruct((HEADS, 2 * LANES, rows), SMALL),
        jax.ShapeDtypeStruct((rows, width), jnp.bfloat16),
    ]
    out_shape = out_shape if want_q else out_shape[1:]
    return pl.pallas_call(
        functools.partial(qkv_kernel, want_q, block),
        in_specs=[in_vmem] * 3,
        out_specs=[in_vmem] * len(out_shape),
        out_shape=out_shape,
        compiler_params=params(12),
        cost_estimate=cost(2 * rows * width * width * (3 if want_q else 2), 6 * rows * width),
        name="space_qkv" if want_q else "space_kv",
    )(x, gain, w)


def attend_kernel(
    block, keys_step, q_ref, kt0, kt1, v0_ref, v1_ref, x_ref, w_ref, o_ref, held, att
):
    rows = x_ref.shape[0]
    half = v0_ref.shape[0]
    steps = 2 * half // keys_step
    pairs = HEADS // 2
    units = rows // block * pairs
    low = lane_is_low((block, LANES))
    ones = jnp.ones((keys_step, LANES), jnp.bfloat16)
    tops = {}

    def place(at):
        unit, step = divmod(at, steps)
        b, pair = divmod(unit, pairs)
        key_at = step % (steps // 2) * keys_step
        return (
            unit,
            step,
            slice(b * block, (b + 1) * block),
            pair,
            slice(pair * LANES, (pair + 1) * LANES),
            step >= steps // 2,
            slice(key_at, key_at + keys_step),
            slice(step * keys_step, (step + 1) * keys_step),
        )

    def score(at):
        unit, step, here, pair, _, second, keys, cols = place(at)
        kt = kt1 if second else kt0
        for odd in range(2):
            scores = dot(q_ref[2 * pair + odd, here], kt[2 * pair + odd, :, keys])
            held[unit % 2, odd * block : (odd + 1) * block, cols] = scores
            top = tops.get((unit, odd))
            for c in range(keys_step // LANES):
                part = scores[:, c * LANES : (c + 1) * LANES]
                top = part if top is None else jnp.maximum(top, part)
            tops[unit, odd] = top if step < steps - 1 else jnp.max(top, axis=-1, keepdims=True)

    def mix(at):
        unit, _, _, _, lanes, second, keys, cols = place(at)
        weights = [
            jnp.exp2(held[unit % 2, odd * block : (odd + 1) * block, cols] - tops[unit, odd])
            for odd in range(2)
        ]
        values = (v1_ref if second else v0_ref)[keys, lanes]
        return dot(
            jnp.concatenate([w.astype(jnp.bfloat16) for w in weights], axis=0),
            jnp.concatenate([values, ones], axis=1),
        )

    for at in range(steps):
        score(at)
    mixed = None
    for at in range(units * steps):
        unit, step, here, pair, lanes, _, _, _ = place(at)
        part = mix(at)
        mixed = mixed + part if step else part
        if at + steps < units * steps:
            score(at + steps)
        if step == steps - 1:
            done = mixed[:, :LANES] / mixed[:, LANES:]
            att[here, lanes] = jnp.where(low, done[:block], done[block:]).astype(jnp.bfloat16)
            if pair == pairs - 1:
                out = x_ref[here, :].astype(jnp.float32) + dot(att[here, :], w_ref[...])
                o_ref[here, :] = out.astype(jnp.bfloat16)


def attend(q, kt0, kt1, v0, v1, x, w, block=512, keys_step=512):
    rows, width = x.shape
    keys = 2 * v0.shape[0]
    in_vmem = pl.BlockSpec(memory_space=pltpu.VMEM)
    return pl.pallas_call(
        functools.partial(attend_kernel, block, keys_step),
        in_specs=[in_vmem] * 7,
        out_specs=in_vmem,
        out_shape=jax.ShapeDtypeStruct((rows, width), jnp.bfloat16),
        scratch_shapes=[
            pltpu.VMEM((2, 2 * block, keys), jnp.float32),
            pltpu.VMEM((rows, width), jnp.bfloat16),
        ],
        compiler_params=params(28),
        cost_estimate=cost(8 * rows * keys * width, 12 * keys * width),
        name="space_attend",
    )(q, kt0, kt1, v0, v1, x, w)


def member_kernel(
    block, mlp_block, ff_step, x_ref, gain_ref, wqkv_ref, wout_ref, gain2_ref, wup_ref, wdown_ref,
    o_ref, rows32, qs, ks, vs, att,
):
    members, tokens, width = x_ref.shape
    ff = wup_ref.shape[1]
    total = members * tokens
    scale = (width // HEADS) ** (-0.5) * SCORE_SCALE
    columns = range(width // LANES)
    flat = x_ref[...].reshape(total, width).astype(jnp.float32)
    for c in columns:
        rows32[c] = flat[:, c * LANES : (c + 1) * LANES]

    def lane_slice(c):
        return slice(c * LANES, (c + 1) * LANES)

    def token_rows(token):
        parts = [rows32[c, pl.ds(token, members, stride=tokens), :] for c in columns]
        return jnp.concatenate(parts, axis=1)

    xs = []
    per_block = block // members
    for b in range(total // block):
        here = slice(b * block, (b + 1) * block)
        x = jnp.concatenate([token_rows(b * per_block + t) for t in range(per_block)], axis=0)
        xs.append(x)
        n = normed(x, gain_ref[...])
        qs[here, :] = (dot(n, wqkv_ref[:, :width]) * scale).astype(jnp.bfloat16)
        ks[here, :] = dot(n, wqkv_ref[:, width : 2 * width]).astype(jnp.bfloat16)
        vs[here, :] = dot(n, wqkv_ref[:, 2 * width :]).astype(jnp.bfloat16)

    tile = 4 * members
    low = lane_is_low((tile, LANES))
    same = (
        lax.broadcasted_iota(jnp.int32, (2 * tile, tile), 0) % tile // members
        == lax.broadcasted_iota(jnp.int32, (2 * tile, tile), 1) // members
    )
    ones = jnp.ones((tile, LANES), jnp.bfloat16)

    def score(rows, lanes):
        queries = qs[rows, lanes]
        none = jnp.zeros_like(queries)
        both = jnp.concatenate(
            [jnp.where(low, queries, none), jnp.where(low, none, queries)], axis=0
        )
        return lax.dot_general(both, ks[rows, lanes], NT, preferred_element_type=jnp.float32)

    work = [
        (slice(g * tile, (g + 1) * tile), lane_slice(pair))
        for g in range(total // tile)
        for pair in range(HEADS // 2)
    ]
    later = score(*work[0])
    for i, (rows, lanes) in enumerate(work):
        scores = jnp.where(same, later, -jnp.inf)
        if i + 1 < len(work):
            later = score(*work[i + 1])
        peaks = jnp.max(scores, axis=-1, keepdims=True)
        weights = jnp.exp2(scores - peaks).astype(jnp.bfloat16)
        mixed = dot(weights, jnp.concatenate([vs[rows, lanes], ones], axis=1))
        done = mixed[:, :LANES] / mixed[:, LANES:]
        att[rows, lanes] = jnp.where(low, done[:tile], done[tile:]).astype(jnp.bfloat16)

    for b in range(total // mlp_block):
        here = slice(b * mlp_block, (b + 1) * mlp_block)
        share = mlp_block // block
        x = jnp.concatenate(xs[b * share : (b + 1) * share], axis=0)
        after = (x + dot(att[here, :], wout_ref[...])).astype(jnp.bfloat16).astype(jnp.float32)
        out = after
        n = normed(after, gain2_ref[...])
        up = dot(n, wup_ref[:, :ff_step])
        for j in range(0, ff, ff_step):
            later = dot(n, wup_ref[:, j + ff_step : j + 2 * ff_step]) if j + ff_step < ff else None
            hidden = jax.nn.gelu(up, approximate=True).astype(jnp.bfloat16)
            out = out + dot(hidden, wdown_ref[j : j + ff_step, :])
            up = later
        for t in range(mlp_block // members):
            token = b * (mlp_block // members) + t
            for c in columns:
                rows32[c, pl.ds(token, members, stride=tokens), :] = out[
                    t * members : (t + 1) * members, lane_slice(c)
                ]
    for c in columns:
        o_ref[:, :, lane_slice(c)] = (
            rows32[c].astype(jnp.bfloat16).reshape(members, tokens, LANES)
        )


def member_part(x, gain, wqkv, wout, gain2, wup, wdown, block=256, mlp_block=512, ff_step=256):
    members, tokens, width = x.shape
    total, ff = members * tokens, wup.shape[1]
    in_vmem = pl.BlockSpec(memory_space=pltpu.VMEM)
    return pl.pallas_call(
        functools.partial(member_kernel, block, mlp_block, ff_step),
        in_specs=[in_vmem] * 7,
        out_specs=in_vmem,
        out_shape=jax.ShapeDtypeStruct((members, tokens, width), jnp.bfloat16),
        scratch_shapes=[pltpu.VMEM((width // LANES, total, LANES), jnp.float32)]
        + [pltpu.VMEM((total, width), jnp.bfloat16)] * 4,
        compiler_params=params(24),
        cost_estimate=cost(total * width * 2 * (4 * width + 2 * ff) * 2, 6 * total * width),
        name="member_part",
    )(x, gain, wqkv, wout, gain2, wup, wdown)


def per_device(
    state_field,
    gain_space,
    w_qkv_space,
    w_out_space,
    gain_member,
    w_qkv_member,
    w_out_member,
    gain_mlp,
    w_up,
    w_down,
):
    mem_dev, tok_dev, width = state_field.shape
    n_mem, n_grp = lax.axis_size("mem"), lax.axis_size("grp")
    gain_space, gain_member, gain_mlp = (g[None] for g in (gain_space, gain_member, gain_mlp))
    with jax.named_scope("tokens_to_member"):
        mine = lax.all_to_all(state_field, "grp", split_axis=0, concat_axis=0, tiled=True)
    x = mine.reshape(n_grp * tok_dev, width)
    with jax.named_scope("rows_of_other_core"):
        x_other = lax.ppermute(x, "core", [(0, 1), (1, 0)])
    q, kt, v = project_qkv(x, gain_space, w_qkv_space, True)
    kt_other, v_other = project_qkv(x_other, gain_space, w_qkv_space, False)
    after_space = attend(q, kt, kt_other, v, v_other, x, w_out_space)
    here = tok_dev // n_mem
    sent = after_space.reshape(n_grp * n_mem, here, width)
    with jax.named_scope("members_to_tokens"):
        tokens = lax.all_to_all(sent, ("grp", "mem"), split_axis=0, concat_axis=0, tiled=True)
    out = member_part(tokens, gain_member, w_qkv_member, w_out_member, gain_mlp, w_up, w_down)
    out = out.reshape(n_grp, n_mem, here, width).transpose(1, 0, 2, 3)
    with jax.named_scope("tokens_back"):
        back = lax.all_to_all(out, "mem", split_axis=0, concat_axis=0, tiled=True)
    return back.transpose(1, 0, 2, 3).reshape(mem_dev, tok_dev, width)


def solution(mesh):
    grid = Mesh(mesh.devices.reshape(8, 8, 2), ("mem", "grp", "core"))
    rows = P("mem", ("grp", "core"), None)
    return jax.shard_map(
        per_device, mesh=grid, in_specs=(rows,) + (P(),) * 9, out_specs=rows, check_vma=False
    )
```

```python
import functools
import math

import jax
import jax.numpy as jnp
from jax import lax
from jax.experimental import pallas as pl
from jax.experimental.pallas import tpu as pltpu
from jax.sharding import Mesh, PartitionSpec as P

HEADS = 8
LANES = 128
SCORE_SCALE = math.log2(math.e)
SMALL = jnp.float8_e4m3fn
NT = (((1,), (1,)), ((), ()))


def params(mib):
    return pltpu.CompilerParams(vmem_limit_bytes=mib * 1024 * 1024)


def cost(flops, moved):
    return pl.CostEstimate(flops=int(flops), bytes_accessed=int(moved), transcendentals=0)


def normed(values, gain):
    scaled = values * lax.rsqrt(jnp.mean(values * values, axis=-1, keepdims=True) + 1e-05)
    return (scaled * gain).astype(jnp.bfloat16)


def dot(a, b):
    return jnp.dot(a, b, preferred_element_type=jnp.float32)


def lane_is_low(shape):
    return lax.broadcasted_iota(jnp.int32, shape, 1) < LANES // 2


def high_low(values):
    high = values.astype(SMALL).astype(jnp.bfloat16)
    return high, values - high


def turned(values):
    return jnp.concatenate([values[:, LANES // 2 :], values[:, : LANES // 2]], axis=1)


def put_queries(q_ref, here, q):
    for pair in range(HEADS // 2):
        high, low_part = high_low(q[:, pair * LANES : (pair + 1) * LANES].astype(jnp.bfloat16))
        low_part = low_part * 4
        quarter = high * 0.25
        first = lane_is_low(high.shape)
        even, odd = 2 * pair, 2 * pair + 1
        q_ref[even, here, :LANES] = jnp.where(first, high, turned(quarter)).astype(SMALL)
        q_ref[even, here, LANES:] = jnp.where(first, low_part, turned(low_part)).astype(SMALL)
        q_ref[odd, here, :LANES] = jnp.where(first, turned(high), quarter).astype(SMALL)
        q_ref[odd, here, LANES:] = jnp.where(first, turned(low_part), low_part).astype(SMALL)


def put_keys(kt_ref, here, k):
    high, low = high_low(k.astype(jnp.bfloat16).T)
    parts = [p.astype(SMALL) for p in (high, low * 4, high * 0.25, low * 0.25)]
    dim = high.shape[0] // HEADS
    for head in range(HEADS):
        for i, part in enumerate(parts):
            kt_ref[head, i * dim : (i + 1) * dim, here] = part[head * dim : (head + 1) * dim]


def even_scales(w_ref, width):
    tiny = 1e-06
    both = SCORE_SCALE * (width // HEADS) ** (-0.5)
    q_norm, k_norm = (
        jnp.sum(jnp.square(w_ref[:, part * width : (part + 1) * width].astype(jnp.float32)), axis=0, keepdims=True)
        for part in range(2)
    )
    root = jnp.sqrt(jnp.sqrt((q_norm + tiny) / (k_norm + tiny)))
    return both**0.5 / root, both**0.5 * root


def qkv_kernel(want_q, block, x_ref, gain_ref, w_ref, *outs):
    total, width = x_ref.shape
    q_scale, k_scale = even_scales(w_ref, width)
    for b in range(total // block):
        here = slice(b * block, (b + 1) * block)
        rows = normed(x_ref[here, :].astype(jnp.float32), gain_ref[...])
        if want_q:
            put_queries(outs[0], here, dot(rows, w_ref[:, :width]) * q_scale)
        put_keys(outs[-2], here, dot(rows, w_ref[:, width : 2 * width]) * k_scale)
        outs[-1][here, :] = dot(rows, w_ref[:, 2 * width :]).astype(jnp.bfloat16)


def project_qkv(x, gain, w, want_q, block=512):
    rows, width = x.shape
    in_vmem = pl.BlockSpec(memory_space=pltpu.VMEM)
    out_shape = [
        jax.ShapeDtypeStruct((HEADS, rows, 2 * LANES), SMALL),
        jax.ShapeDtypeStruct((HEADS, 2 * LANES, rows), SMALL),
        jax.ShapeDtypeStruct((rows, width), jnp.bfloat16),
    ]
    out_shape = out_shape if want_q else out_shape[1:]
    return pl.pallas_call(
        functools.partial(qkv_kernel, want_q, block),
        in_specs=[in_vmem] * 3,
        out_specs=[in_vmem] * len(out_shape),
        out_shape=out_shape,
        compiler_params=params(12),
        cost_estimate=cost(2 * rows * width * width * (3 if want_q else 2), 6 * rows * width),
        name="space_qkv" if want_q else "space_kv",
    )(x, gain, w)


def attend_kernel(
    block, keys_step, q_ref, kt0, kt1, v0_ref, v1_ref, x_ref, w_ref, o_ref, held, att
):
    rows = x_ref.shape[0]
    half = v0_ref.shape[0]
    steps = 2 * half // keys_step
    pairs = HEADS // 2
    units = rows // block * pairs
    low = lane_is_low((block, LANES))
    ones = jnp.ones((keys_step, LANES), jnp.bfloat16)
    tops = {}

    def place(at):
        unit, step = divmod(at, steps)
        b, pair = divmod(unit, pairs)
        key_at = step % (steps // 2) * keys_step
        return (
            unit,
            step,
            slice(b * block, (b + 1) * block),
            pair,
            slice(pair * LANES, (pair + 1) * LANES),
            step >= steps // 2,
            slice(key_at, key_at + keys_step),
            slice(step * keys_step, (step + 1) * keys_step),
        )

    def score(at):
        unit, step, here, pair, _, second, keys, cols = place(at)
        kt = kt1 if second else kt0
        for odd in range(2):
            scores = dot(q_ref[2 * pair + odd, here], kt[2 * pair + odd, :, keys])
            held[unit % 2, odd * block : (odd + 1) * block, cols] = scores
            top = tops.get((unit, odd))
            for c in range(keys_step // LANES):
                part = scores[:, c * LANES : (c + 1) * LANES]
                top = part if top is None else jnp.maximum(top, part)
            tops[unit, odd] = top if step < steps - 1 else jnp.max(top, axis=-1, keepdims=True)

    def mix(at):
        unit, _, _, _, lanes, second, keys, cols = place(at)
        weights = [
            jnp.exp2(held[unit % 2, odd * block : (odd + 1) * block, cols] - tops[unit, odd])
            for odd in range(2)
        ]
        values = (v1_ref if second else v0_ref)[keys, lanes]
        return dot(
            jnp.concatenate([w.astype(jnp.bfloat16) for w in weights], axis=0),
            jnp.concatenate([values, ones], axis=1),
        )

    for at in range(steps):
        score(at)
    mixed = None
    for at in range(units * steps):
        unit, step, here, pair, lanes, _, _, _ = place(at)
        part = mix(at)
        mixed = mixed + part if step else part
        if at + steps < units * steps:
            score(at + steps)
        if step == steps - 1:
            done = mixed[:, :LANES] / mixed[:, LANES:]
            att[here, lanes] = jnp.where(low, done[:block], done[block:]).astype(jnp.bfloat16)
            if pair == pairs - 1:
                out = x_ref[here, :].astype(jnp.float32) + dot(att[here, :], w_ref[...])
                o_ref[here, :] = out.astype(jnp.bfloat16)


def attend(q, kt0, kt1, v0, v1, x, w, block=512, keys_step=512):
    rows, width = x.shape
    keys = 2 * v0.shape[0]
    in_vmem = pl.BlockSpec(memory_space=pltpu.VMEM)
    return pl.pallas_call(
        functools.partial(attend_kernel, block, keys_step),
        in_specs=[in_vmem] * 7,
        out_specs=in_vmem,
        out_shape=jax.ShapeDtypeStruct((rows, width), jnp.bfloat16),
        scratch_shapes=[
            pltpu.VMEM((2, 2 * block, keys), jnp.float32),
            pltpu.VMEM((rows, width), jnp.bfloat16),
        ],
        compiler_params=params(28),
        cost_estimate=cost(8 * rows * keys * width, 12 * keys * width),
        name="space_attend",
    )(q, kt0, kt1, v0, v1, x, w)


def member_kernel(
    block, mlp_block, ff_step, x_ref, gain_ref, wqkv_ref, wout_ref, gain2_ref, wup_ref, wdown_ref,
    o_ref, rows32, qs, ks, vs, att,
):
    members, tokens, width = x_ref.shape
    ff = wup_ref.shape[1]
    total = members * tokens
    scale = (width // HEADS) ** (-0.5) * SCORE_SCALE
    columns = range(width // LANES)
    flat = x_ref[...].reshape(total, width).astype(jnp.float32)
    for c in columns:
        rows32[c] = flat[:, c * LANES : (c + 1) * LANES]

    def lane_slice(c):
        return slice(c * LANES, (c + 1) * LANES)

    def token_rows(token):
        parts = [rows32[c, pl.ds(token, members, stride=tokens), :] for c in columns]
        return jnp.concatenate(parts, axis=1)

    xs = []
    per_block = block // members
    for b in range(total // block):
        here = slice(b * block, (b + 1) * block)
        x = jnp.concatenate([token_rows(b * per_block + t) for t in range(per_block)], axis=0)
        xs.append(x)
        n = normed(x, gain_ref[...])
        qs[here, :] = (dot(n, wqkv_ref[:, :width]) * scale).astype(jnp.bfloat16)
        ks[here, :] = dot(n, wqkv_ref[:, width : 2 * width]).astype(jnp.bfloat16)
        vs[here, :] = dot(n, wqkv_ref[:, 2 * width :]).astype(jnp.bfloat16)

    tile = 4 * members
    low = lane_is_low((tile, LANES))
    same = (
        lax.broadcasted_iota(jnp.int32, (2 * tile, tile), 0) % tile // members
        == lax.broadcasted_iota(jnp.int32, (2 * tile, tile), 1) // members
    )
    ones = jnp.ones((tile, LANES), jnp.bfloat16)

    def score(rows, lanes):
        queries = qs[rows, lanes]
        none = jnp.zeros_like(queries)
        both = jnp.concatenate(
            [jnp.where(low, queries, none), jnp.where(low, none, queries)], axis=0
        )
        return lax.dot_general(both, ks[rows, lanes], NT, preferred_element_type=jnp.float32)

    work = [
        (slice(g * tile, (g + 1) * tile), lane_slice(pair))
        for g in range(total // tile)
        for pair in range(HEADS // 2)
    ]
    later = score(*work[0])
    for i, (rows, lanes) in enumerate(work):
        scores = jnp.where(same, later, -jnp.inf)
        if i + 1 < len(work):
            later = score(*work[i + 1])
        peaks = jnp.max(scores, axis=-1, keepdims=True)
        weights = jnp.exp2(scores - peaks).astype(jnp.bfloat16)
        mixed = dot(weights, jnp.concatenate([vs[rows, lanes], ones], axis=1))
        done = mixed[:, :LANES] / mixed[:, LANES:]
        att[rows, lanes] = jnp.where(low, done[:tile], done[tile:]).astype(jnp.bfloat16)

    for b in range(total // mlp_block):
        here = slice(b * mlp_block, (b + 1) * mlp_block)
        share = mlp_block // block
        x = jnp.concatenate(xs[b * share : (b + 1) * share], axis=0)
        after = (x + dot(att[here, :], wout_ref[...])).astype(jnp.bfloat16).astype(jnp.float32)
        out = after
        n = normed(after, gain2_ref[...])
        up = dot(n, wup_ref[:, :ff_step])
        for j in range(0, ff, ff_step):
            later = dot(n, wup_ref[:, j + ff_step : j + 2 * ff_step]) if j + ff_step < ff else None
            hidden = jax.nn.gelu(up, approximate=True).astype(jnp.bfloat16)
            out = out + dot(hidden, wdown_ref[j : j + ff_step, :])
            up = later
        for t in range(mlp_block // members):
            token = b * (mlp_block // members) + t
            for c in columns:
                rows32[c, pl.ds(token, members, stride=tokens), :] = out[
                    t * members : (t + 1) * members, lane_slice(c)
                ]
    for c in columns:
        o_ref[:, :, lane_slice(c)] = (
            rows32[c].astype(jnp.bfloat16).reshape(members, tokens, LANES)
        )


def member_part(x, gain, wqkv, wout, gain2, wup, wdown, block=256, mlp_block=512, ff_step=256):
    members, tokens, width = x.shape
    total, ff = members * tokens, wup.shape[1]
    in_vmem = pl.BlockSpec(memory_space=pltpu.VMEM)
    return pl.pallas_call(
        functools.partial(member_kernel, block, mlp_block, ff_step),
        in_specs=[in_vmem] * 7,
        out_specs=in_vmem,
        out_shape=jax.ShapeDtypeStruct((members, tokens, width), jnp.bfloat16),
        scratch_shapes=[pltpu.VMEM((width // LANES, total, LANES), jnp.float32)]
        + [pltpu.VMEM((total, width), jnp.bfloat16)] * 4,
        compiler_params=params(24),
        cost_estimate=cost(total * width * 2 * (4 * width + 2 * ff) * 2, 6 * total * width),
        name="member_part",
    )(x, gain, wqkv, wout, gain2, wup, wdown)


def per_device(
    state_field,
    gain_space,
    w_qkv_space,
    w_out_space,
    gain_member,
    w_qkv_member,
    w_out_member,
    gain_mlp,
    w_up,
    w_down,
):
    mem_dev, tok_dev, width = state_field.shape
    n_mem, n_grp = lax.axis_size("mem"), lax.axis_size("grp")
    gain_space, gain_member, gain_mlp = (g[None] for g in (gain_space, gain_member, gain_mlp))
    with jax.named_scope("tokens_to_member"):
        mine = lax.all_to_all(state_field, "grp", split_axis=0, concat_axis=0, tiled=True)
    x = mine.reshape(n_grp * tok_dev, width)
    with jax.named_scope("rows_of_other_core"):
        x_other = lax.ppermute(x, "core", [(0, 1), (1, 0)])
    q, kt, v = project_qkv(x, gain_space, w_qkv_space, True)
    kt_other, v_other = project_qkv(x_other, gain_space, w_qkv_space, False)
    after_space = attend(q, kt, kt_other, v, v_other, x, w_out_space)
    here = tok_dev // n_mem
    sent = after_space.reshape(n_grp * n_mem, here, width)
    with jax.named_scope("members_to_tokens"):
        tokens = lax.all_to_all(sent, ("grp", "mem"), split_axis=0, concat_axis=0, tiled=True)
    out = member_part(tokens, gain_member, w_qkv_member, w_out_member, gain_mlp, w_up, w_down)
    out = out.reshape(n_grp, n_mem, here, width).transpose(1, 0, 2, 3)
    with jax.named_scope("tokens_back"):
        back = lax.all_to_all(out, "mem", split_axis=0, concat_axis=0, tiled=True)
    return back.transpose(1, 0, 2, 3).reshape(mem_dev, tok_dev, width)


def solution(mesh):
    grid = Mesh(mesh.devices.reshape(8, 8, 2), ("mem", "grp", "core"))
    rows = P("mem", ("grp", "core"), None)
    return jax.shard_map(
        per_device, mesh=grid, in_specs=(rows,) + (P(),) * 9, out_specs=rows, check_vma=False
    )
```

```python
import functools
import math

import jax
import jax.numpy as jnp
from jax import lax
from jax.experimental import pallas as pl
from jax.experimental.pallas import tpu as pltpu
from jax.sharding import Mesh, PartitionSpec as P

HEADS = 8
LANES = 128
SCORE_SCALE = math.log2(math.e)
SMALL = jnp.float8_e4m3fn
NT = (((1,), (1,)), ((), ()))


def params(mib):
    return pltpu.CompilerParams(vmem_limit_bytes=mib * 1024 * 1024)


def cost(flops, moved):
    return pl.CostEstimate(flops=int(flops), bytes_accessed=int(moved), transcendentals=0)


def normed(values, gain):
    scaled = values * lax.rsqrt(jnp.mean(values * values, axis=-1, keepdims=True) + 1e-05)
    return (scaled * gain).astype(jnp.bfloat16)


def dot(a, b):
    return jnp.dot(a, b, preferred_element_type=jnp.float32)


def lane_is_low(shape):
    return lax.broadcasted_iota(jnp.int32, shape, 1) < LANES // 2


def high_low(values):
    high = values.astype(SMALL).astype(jnp.bfloat16)
    return high, values - high


def turned(values):
    return jnp.concatenate([values[:, LANES // 2 :], values[:, : LANES // 2]], axis=1)


def put_queries(q_ref, here, q):
    for pair in range(HEADS // 2):
        high, low_part = high_low(q[:, pair * LANES : (pair + 1) * LANES].astype(jnp.bfloat16))
        low_part = low_part * 4
        quarter = high * 0.25
        first = lane_is_low(high.shape)
        even, odd = 2 * pair, 2 * pair + 1
        q_ref[even, here, :LANES] = jnp.where(first, high, turned(quarter)).astype(SMALL)
        q_ref[even, here, LANES:] = jnp.where(first, low_part, turned(low_part)).astype(SMALL)
        q_ref[odd, here, :LANES] = jnp.where(first, turned(high), quarter).astype(SMALL)
        q_ref[odd, here, LANES:] = jnp.where(first, turned(low_part), low_part).astype(SMALL)


def put_keys(kt_ref, here, k):
    high, low = high_low(k.astype(jnp.bfloat16).T)
    parts = [p.astype(SMALL) for p in (high, low * 4, high * 0.25, low * 0.25)]
    dim = high.shape[0] // HEADS
    for head in range(HEADS):
        for i, part in enumerate(parts):
            kt_ref[head, i * dim : (i + 1) * dim, here] = part[head * dim : (head + 1) * dim]


def even_scales(w_ref, width):
    tiny = 1e-06
    both = SCORE_SCALE * (width // HEADS) ** (-0.5)
    q_norm, k_norm = (
        jnp.sum(jnp.square(w_ref[:, part * width : (part + 1) * width].astype(jnp.float32)), axis=0, keepdims=True)
        for part in range(2)
    )
    root = jnp.sqrt(jnp.sqrt((q_norm + tiny) / (k_norm + tiny)))
    return both**0.5 / root, both**0.5 * root


def qkv_kernel(want_q, block, x_ref, gain_ref, w_ref, *outs):
    total, width = x_ref.shape
    q_scale, k_scale = even_scales(w_ref, width)
    for b in range(total // block):
        here = slice(b * block, (b + 1) * block)
        rows = normed(x_ref[here, :].astype(jnp.float32), gain_ref[...])
        if want_q:
            put_queries(outs[0], here, dot(rows, w_ref[:, :width]) * q_scale)
        put_keys(outs[-2], here, dot(rows, w_ref[:, width : 2 * width]) * k_scale)
        outs[-1][here, :] = dot(rows, w_ref[:, 2 * width :]).astype(jnp.bfloat16)


def project_qkv(x, gain, w, want_q, block=512):
    rows, width = x.shape
    in_vmem = pl.BlockSpec(memory_space=pltpu.VMEM)
    out_shape = [
        jax.ShapeDtypeStruct((HEADS, rows, 2 * LANES), SMALL),
        jax.ShapeDtypeStruct((HEADS, 2 * LANES, rows), SMALL),
        jax.ShapeDtypeStruct((rows, width), jnp.bfloat16),
    ]
    out_shape = out_shape if want_q else out_shape[1:]
    return pl.pallas_call(
        functools.partial(qkv_kernel, want_q, block),
        in_specs=[in_vmem] * 3,
        out_specs=[in_vmem] * len(out_shape),
        out_shape=out_shape,
        compiler_params=params(12),
        cost_estimate=cost(2 * rows * width * width * (3 if want_q else 2), 6 * rows * width),
        name="space_qkv" if want_q else "space_kv",
    )(x, gain, w)


def attend_kernel(
    block, keys_step, q_ref, kt0, kt1, v0_ref, v1_ref, x_ref, w_ref, o_ref, held, att
):
    rows = x_ref.shape[0]
    half = v0_ref.shape[0]
    steps = 2 * half // keys_step
    pairs = HEADS // 2
    units = rows // block * pairs
    low = lane_is_low((block, LANES))
    ones = jnp.ones((keys_step, LANES), jnp.bfloat16)
    tops = {}

    def place(at):
        unit, step = divmod(at, steps)
        b, pair = divmod(unit, pairs)
        key_at = step % (steps // 2) * keys_step
        return (
            unit,
            step,
            slice(b * block, (b + 1) * block),
            pair,
            slice(pair * LANES, (pair + 1) * LANES),
            step >= steps // 2,
            slice(key_at, key_at + keys_step),
            slice(step * keys_step, (step + 1) * keys_step),
        )

    def score(at):
        unit, step, here, pair, _, second, keys, cols = place(at)
        kt = kt1 if second else kt0
        for odd in range(2):
            scores = dot(q_ref[2 * pair + odd, here], kt[2 * pair + odd, :, keys])
            held[unit % 2, odd * block : (odd + 1) * block, cols] = scores
            top = tops.get((unit, odd))
            for c in range(keys_step // LANES):
                part = scores[:, c * LANES : (c + 1) * LANES]
                top = part if top is None else jnp.maximum(top, part)
            tops[unit, odd] = top if step < steps - 1 else jnp.max(top, axis=-1, keepdims=True)

    def mix(at):
        unit, _, _, _, lanes, second, keys, cols = place(at)
        weights = [
            jnp.exp2(held[unit % 2, odd * block : (odd + 1) * block, cols] - tops[unit, odd])
            for odd in range(2)
        ]
        values = (v1_ref if second else v0_ref)[keys, lanes]
        return dot(
            jnp.concatenate([w.astype(jnp.bfloat16) for w in weights], axis=0),
            jnp.concatenate([values, ones], axis=1),
        )

    for at in range(steps):
        score(at)
    mixed = None
    for at in range(units * steps):
        unit, step, here, pair, lanes, _, _, _ = place(at)
        part = mix(at)
        mixed = mixed + part if step else part
        if at + steps < units * steps:
            score(at + steps)
        if step == steps - 1:
            done = mixed[:, :LANES] / mixed[:, LANES:]
            att[here, lanes] = jnp.where(low, done[:block], done[block:]).astype(jnp.bfloat16)
            if pair == pairs - 1:
                out = x_ref[here, :].astype(jnp.float32) + dot(att[here, :], w_ref[...])
                out = out.astype(jnp.bfloat16)
                n_xh, n_z, n_xl, n_y, tokens, _ = o_ref.shape
                pieces = block // tokens
                for i in range(pieces):
                    piece = at // steps // pairs * pieces + i
                    xh, z = divmod(piece // (n_y * n_xl), n_z)
                    y, xl = divmod(piece % (n_y * n_xl), n_xl)
                    o_ref[xh, z, xl, y] = out[i * tokens : (i + 1) * tokens]


def attend(q, kt0, kt1, v0, v1, x, w, order, block=512, keys_step=512):
    rows, width = x.shape
    keys = 2 * v0.shape[0]
    in_vmem = pl.BlockSpec(memory_space=pltpu.VMEM)
    return pl.pallas_call(
        functools.partial(attend_kernel, block, keys_step),
        in_specs=[in_vmem] * 7,
        out_specs=in_vmem,
        out_shape=jax.ShapeDtypeStruct(order + (rows // math.prod(order), width), jnp.bfloat16),
        scratch_shapes=[
            pltpu.VMEM((2, 2 * block, keys), jnp.float32),
            pltpu.VMEM((rows, width), jnp.bfloat16),
        ],
        compiler_params=params(28),
        cost_estimate=cost(8 * rows * keys * width, 12 * keys * width),
        name="space_attend",
    )(q, kt0, kt1, v0, v1, x, w)


def member_kernel(
    block, mlp_block, ff_step, x_ref, gain_ref, wqkv_ref, wout_ref, gain2_ref, wup_ref, wdown_ref,
    o_ref, rows32, qs, ks, vs, att,
):
    members, tokens, width = x_ref.shape
    ff = wup_ref.shape[1]
    total = members * tokens
    scale = (width // HEADS) ** (-0.5) * SCORE_SCALE
    columns = range(width // LANES)
    flat = x_ref[...].reshape(total, width).astype(jnp.float32)
    for c in columns:
        rows32[c] = flat[:, c * LANES : (c + 1) * LANES]

    def lane_slice(c):
        return slice(c * LANES, (c + 1) * LANES)

    def token_rows(token):
        parts = [rows32[c, pl.ds(token, members, stride=tokens), :] for c in columns]
        return jnp.concatenate(parts, axis=1)

    xs = []
    per_block = block // members
    for b in range(total // block):
        here = slice(b * block, (b + 1) * block)
        x = jnp.concatenate([token_rows(b * per_block + t) for t in range(per_block)], axis=0)
        xs.append(x)
        n = normed(x, gain_ref[...])
        qs[here, :] = (dot(n, wqkv_ref[:, :width]) * scale).astype(jnp.bfloat16)
        ks[here, :] = dot(n, wqkv_ref[:, width : 2 * width]).astype(jnp.bfloat16)
        vs[here, :] = dot(n, wqkv_ref[:, 2 * width :]).astype(jnp.bfloat16)

    tile = 4 * members
    low = lane_is_low((tile, LANES))
    same = (
        lax.broadcasted_iota(jnp.int32, (2 * tile, tile), 0) % tile // members
        == lax.broadcasted_iota(jnp.int32, (2 * tile, tile), 1) // members
    )
    ones = jnp.ones((tile, LANES), jnp.bfloat16)

    def score(rows, lanes):
        queries = qs[rows, lanes]
        none = jnp.zeros_like(queries)
        both = jnp.concatenate(
            [jnp.where(low, queries, none), jnp.where(low, none, queries)], axis=0
        )
        return lax.dot_general(both, ks[rows, lanes], NT, preferred_element_type=jnp.float32)

    work = [
        (slice(g * tile, (g + 1) * tile), lane_slice(pair))
        for g in range(total // tile)
        for pair in range(HEADS // 2)
    ]
    later = score(*work[0])
    for i, (rows, lanes) in enumerate(work):
        scores = jnp.where(same, later, -jnp.inf)
        if i + 1 < len(work):
            later = score(*work[i + 1])
        peaks = jnp.max(scores, axis=-1, keepdims=True)
        weights = jnp.exp2(scores - peaks).astype(jnp.bfloat16)
        mixed = dot(weights, jnp.concatenate([vs[rows, lanes], ones], axis=1))
        done = mixed[:, :LANES] / mixed[:, LANES:]
        att[rows, lanes] = jnp.where(low, done[:tile], done[tile:]).astype(jnp.bfloat16)

    for b in range(total // mlp_block):
        here = slice(b * mlp_block, (b + 1) * mlp_block)
        share = mlp_block // block
        x = jnp.concatenate(xs[b * share : (b + 1) * share], axis=0)
        after = (x + dot(att[here, :], wout_ref[...])).astype(jnp.bfloat16).astype(jnp.float32)
        out = after
        n = normed(after, gain2_ref[...])
        up = dot(n, wup_ref[:, :ff_step])
        for j in range(0, ff, ff_step):
            later = dot(n, wup_ref[:, j + ff_step : j + 2 * ff_step]) if j + ff_step < ff else None
            hidden = jax.nn.gelu(up, approximate=True).astype(jnp.bfloat16)
            out = out + dot(hidden, wdown_ref[j : j + ff_step, :])
            up = later
        for t in range(mlp_block // members):
            token = b * (mlp_block // members) + t
            for c in columns:
                rows32[c, pl.ds(token, members, stride=tokens), :] = out[
                    t * members : (t + 1) * members, lane_slice(c)
                ]
    for c in columns:
        o_ref[:, :, lane_slice(c)] = (
            rows32[c].astype(jnp.bfloat16).reshape(members, tokens, LANES)
        )


def member_part(x, gain, wqkv, wout, gain2, wup, wdown, block=256, mlp_block=512, ff_step=256):
    members, tokens, width = x.shape
    total, ff = members * tokens, wup.shape[1]
    in_vmem = pl.BlockSpec(memory_space=pltpu.VMEM)
    return pl.pallas_call(
        functools.partial(member_kernel, block, mlp_block, ff_step),
        in_specs=[in_vmem] * 7,
        out_specs=in_vmem,
        out_shape=jax.ShapeDtypeStruct((members, tokens, width), jnp.bfloat16),
        scratch_shapes=[pltpu.VMEM((width // LANES, total, LANES), jnp.float32)]
        + [pltpu.VMEM((total, width), jnp.bfloat16)] * 4,
        compiler_params=params(24),
        cost_estimate=cost(total * width * 2 * (4 * width + 2 * ff) * 2, 6 * total * width),
        name="member_part",
    )(x, gain, wqkv, wout, gain2, wup, wdown)


def per_device(
    state_field,
    gain_space,
    w_qkv_space,
    w_out_space,
    gain_member,
    w_qkv_member,
    w_out_member,
    gain_mlp,
    w_up,
    w_down,
):
    mem_dev, tok_dev, width = state_field.shape
    n_y, n_xl, n_z, n_xh = (lax.axis_size(name) for name in ("y", "xl", "z", "xh"))
    gain_space, gain_member, gain_mlp = (g[None] for g in (gain_space, gain_member, gain_mlp))
    with jax.named_scope("tokens_to_member"):
        mine = lax.all_to_all(state_field, ("xh", "z"), split_axis=0, concat_axis=0, tiled=True)
    x = mine.reshape(n_xh * n_z * tok_dev, width)
    with jax.named_scope("rows_of_other_core"):
        x_other = lax.ppermute(x, "core", [(0, 1), (1, 0)])
    q, kt, v = project_qkv(x, gain_space, w_qkv_space, True)
    kt_other, v_other = project_qkv(x_other, gain_space, w_qkv_space, False)
    order = (n_xh, n_z, n_xl, n_y)
    after_space = attend(q, kt, kt_other, v, v_other, x, w_out_space, order)
    here = tok_dev // (n_y * n_xl)
    sent = after_space.reshape(math.prod(order), here, width)
    with jax.named_scope("members_to_tokens"):
        tokens = lax.all_to_all(
            sent, ("xh", "z", "xl", "y"), split_axis=0, concat_axis=0, tiled=True
        )
    out = member_part(tokens, gain_member, w_qkv_member, w_out_member, gain_mlp, w_up, w_down)
    out = out.reshape(n_xh * n_z, n_xl * n_y, here, width).transpose(1, 0, 2, 3)
    with jax.named_scope("tokens_back"):
        back = lax.all_to_all(out, ("xl", "y"), split_axis=0, concat_axis=0, tiled=True)
    back = back.reshape(n_xl, n_y, n_xh, n_z, here, width).transpose(2, 3, 1, 0, 4, 5)
    return back.reshape(mem_dev, tok_dev, width)


def solution(mesh):
    grid = Mesh(mesh.devices.reshape(4, 2, 4, 2, 2), ("y", "xl", "z", "xh", "core"))
    rows = P(("y", "xl"), ("z", "xh", "core"), None)
    return jax.shard_map(
        per_device, mesh=grid, in_specs=(rows,) + (P(),) * 9, out_specs=rows, check_vma=False
    )
```

```python
import functools
import math

import jax
import jax.numpy as jnp
from jax import lax
from jax.experimental import pallas as pl
from jax.experimental.pallas import tpu as pltpu
from jax.sharding import Mesh, PartitionSpec as P

HEADS = 8
LANES = 128
SCORE_SCALE = math.log2(math.e)
SMALL = jnp.float8_e4m3fn
NT = (((1,), (1,)), ((), ()))


def params(mib):
    return pltpu.CompilerParams(vmem_limit_bytes=mib * 1024 * 1024)


def cost(flops, moved):
    return pl.CostEstimate(flops=int(flops), bytes_accessed=int(moved), transcendentals=0)


def normed(values, gain):
    scaled = values * lax.rsqrt(jnp.mean(values * values, axis=-1, keepdims=True) + 1e-05)
    return (scaled * gain).astype(jnp.bfloat16)


def gelu(x):
    c = (2 / math.pi) ** 0.5
    half = 0.5 * x
    return half + half * jnp.tanh(x * (c + (c * 0.044715) * (x * x)))


def dot(a, b):
    return jnp.dot(a, b, preferred_element_type=jnp.float32)


def lane_is_low(shape):
    return lax.broadcasted_iota(jnp.int32, shape, 1) < LANES // 2


def high_low(values):
    high = values.astype(SMALL).astype(jnp.bfloat16)
    return high, values - high


def turned(values):
    return jnp.concatenate([values[:, LANES // 2 :], values[:, : LANES // 2]], axis=1)


def put_queries(q_ref, here, q):
    for pair in range(HEADS // 2):
        high, low_part = high_low(q[:, pair * LANES : (pair + 1) * LANES].astype(jnp.bfloat16))
        low_part = low_part * 4
        quarter = high * 0.25
        first = lane_is_low(high.shape)
        even, odd = 2 * pair, 2 * pair + 1
        q_ref[even, here, :LANES] = jnp.where(first, high, turned(quarter)).astype(SMALL)
        q_ref[even, here, LANES:] = jnp.where(first, low_part, turned(low_part)).astype(SMALL)
        q_ref[odd, here, :LANES] = jnp.where(first, turned(high), quarter).astype(SMALL)
        q_ref[odd, here, LANES:] = jnp.where(first, turned(low_part), low_part).astype(SMALL)


def put_keys(kt_ref, here, k):
    high, low = high_low(k.astype(jnp.bfloat16).T)
    parts = [p.astype(SMALL) for p in (high, low * 4, high * 0.25, low * 0.25)]
    dim = high.shape[0] // HEADS
    for head in range(HEADS):
        for i, part in enumerate(parts):
            kt_ref[head, i * dim : (i + 1) * dim, here] = part[head * dim : (head + 1) * dim]


def even_scales(w_ref, width):
    tiny = 1e-06
    both = SCORE_SCALE * (width // HEADS) ** (-0.5)
    q_norm, k_norm = (
        jnp.sum(jnp.square(w_ref[:, part * width : (part + 1) * width].astype(jnp.float32)), axis=0, keepdims=True)
        for part in range(2)
    )
    root = jnp.sqrt(jnp.sqrt((q_norm + tiny) / (k_norm + tiny)))
    return both**0.5 / root, both**0.5 * root


def qkv_kernel(want_q, block, x_ref, gain_ref, w_ref, *outs):
    total, width = x_ref.shape
    q_scale, k_scale = even_scales(w_ref, width)
    for b in range(total // block):
        here = slice(b * block, (b + 1) * block)
        rows = normed(x_ref[here, :].astype(jnp.float32), gain_ref[...])
        if want_q:
            put_queries(outs[0], here, dot(rows, w_ref[:, :width]) * q_scale)
        put_keys(outs[-2], here, dot(rows, w_ref[:, width : 2 * width]) * k_scale)
        outs[-1][here, :] = dot(rows, w_ref[:, 2 * width :]).astype(jnp.bfloat16)


def project_qkv(x, gain, w, want_q, block=512):
    rows, width = x.shape
    in_vmem = pl.BlockSpec(memory_space=pltpu.VMEM)
    out_shape = [
        jax.ShapeDtypeStruct((HEADS, rows, 2 * LANES), SMALL),
        jax.ShapeDtypeStruct((HEADS, 2 * LANES, rows), SMALL),
        jax.ShapeDtypeStruct((rows, width), jnp.bfloat16),
    ]
    out_shape = out_shape if want_q else out_shape[1:]
    return pl.pallas_call(
        functools.partial(qkv_kernel, want_q, block),
        in_specs=[in_vmem] * 3,
        out_specs=[in_vmem] * len(out_shape),
        out_shape=out_shape,
        compiler_params=params(12),
        cost_estimate=cost(2 * rows * width * width * (3 if want_q else 2), 6 * rows * width),
        name="space_qkv" if want_q else "space_kv",
    )(x, gain, w)


def attend_kernel(
    block, keys_step, q_ref, kt0, kt1, v0_ref, v1_ref, x_ref, w_ref, o_ref, held, att
):
    rows = x_ref.shape[0]
    half = v0_ref.shape[0]
    steps = 2 * half // keys_step
    pairs = HEADS // 2
    units = rows // block * pairs
    low = lane_is_low((block, LANES))
    ones = jnp.ones((keys_step, LANES), jnp.bfloat16)
    tops = {}

    def place(at):
        unit, step = divmod(at, steps)
        b, pair = divmod(unit, pairs)
        key_at = step % (steps // 2) * keys_step
        return (
            unit,
            step,
            slice(b * block, (b + 1) * block),
            pair,
            slice(pair * LANES, (pair + 1) * LANES),
            step >= steps // 2,
            slice(key_at, key_at + keys_step),
            slice(step * keys_step, (step + 1) * keys_step),
        )

    def score(at):
        unit, step, here, pair, _, second, keys, cols = place(at)
        kt = kt1 if second else kt0
        for odd in range(2):
            scores = dot(q_ref[2 * pair + odd, here], kt[2 * pair + odd, :, keys])
            held[unit % 2, odd * block : (odd + 1) * block, cols] = scores
            top = tops.get((unit, odd))
            for c in range(keys_step // LANES):
                part = scores[:, c * LANES : (c + 1) * LANES]
                top = part if top is None else jnp.maximum(top, part)
            tops[unit, odd] = top if step < steps - 1 else jnp.max(top, axis=-1, keepdims=True)

    def mix(at):
        unit, _, _, _, lanes, second, keys, cols = place(at)
        weights = [
            jnp.exp2(held[unit % 2, odd * block : (odd + 1) * block, cols] - tops[unit, odd])
            for odd in range(2)
        ]
        values = (v1_ref if second else v0_ref)[keys, lanes]
        return dot(
            jnp.concatenate([w.astype(jnp.bfloat16) for w in weights], axis=0),
            jnp.concatenate([values, ones], axis=1),
        )

    for at in range(steps):
        score(at)
    mixed = None
    for at in range(units * steps):
        unit, step, here, pair, lanes, _, _, _ = place(at)
        part = mix(at)
        mixed = mixed + part if step else part
        if at + steps < units * steps:
            score(at + steps)
        if step == steps - 1:
            done = mixed[:, :LANES] / mixed[:, LANES:]
            att[here, lanes] = jnp.where(low, done[:block], done[block:]).astype(jnp.bfloat16)
            if pair == pairs - 1:
                out = x_ref[here, :].astype(jnp.float32) + dot(att[here, :], w_ref[...])
                out = out.astype(jnp.bfloat16)
                n_xh, n_z, n_xl, n_y, tokens, _ = o_ref.shape
                pieces = block // tokens
                for i in range(pieces):
                    piece = at // steps // pairs * pieces + i
                    xh, z = divmod(piece // (n_y * n_xl), n_z)
                    y, xl = divmod(piece % (n_y * n_xl), n_xl)
                    o_ref[xh, z, xl, y] = out[i * tokens : (i + 1) * tokens]


def attend(q, kt0, kt1, v0, v1, x, w, order, block=512, keys_step=512):
    rows, width = x.shape
    keys = 2 * v0.shape[0]
    in_vmem = pl.BlockSpec(memory_space=pltpu.VMEM)
    return pl.pallas_call(
        functools.partial(attend_kernel, block, keys_step),
        in_specs=[in_vmem] * 7,
        out_specs=in_vmem,
        out_shape=jax.ShapeDtypeStruct(order + (rows // math.prod(order), width), jnp.bfloat16),
        scratch_shapes=[
            pltpu.VMEM((2, 2 * block, keys), jnp.float32),
            pltpu.VMEM((rows, width), jnp.bfloat16),
        ],
        compiler_params=params(28),
        cost_estimate=cost(8 * rows * keys * width, 12 * keys * width),
        name="space_attend",
    )(q, kt0, kt1, v0, v1, x, w)


def member_kernel(
    block, mlp_block, ff_step, x_ref, gain_ref, wqkv_ref, wout_ref, gain2_ref, wup_ref, wdown_ref,
    o_ref, rows32, qs, ks, vs, att,
):
    members, tokens, width = x_ref.shape
    ff = wup_ref.shape[1]
    total = members * tokens
    scale = (width // HEADS) ** (-0.5) * SCORE_SCALE
    columns = range(width // LANES)
    flat = x_ref[...].reshape(total, width).astype(jnp.float32)
    for c in columns:
        rows32[c] = flat[:, c * LANES : (c + 1) * LANES]

    def lane_slice(c):
        return slice(c * LANES, (c + 1) * LANES)

    def token_rows(token):
        parts = [rows32[c, pl.ds(token, members, stride=tokens), :] for c in columns]
        return jnp.concatenate(parts, axis=1)

    xs = []
    per_block = block // members
    for b in range(total // block):
        here = slice(b * block, (b + 1) * block)
        x = jnp.concatenate([token_rows(b * per_block + t) for t in range(per_block)], axis=0)
        xs.append(x)
        n = normed(x, gain_ref[...])
        qs[here, :] = (dot(n, wqkv_ref[:, :width]) * scale).astype(jnp.bfloat16)
        ks[here, :] = dot(n, wqkv_ref[:, width : 2 * width]).astype(jnp.bfloat16)
        vs[here, :] = dot(n, wqkv_ref[:, 2 * width :]).astype(jnp.bfloat16)

    tile = 4 * members
    low = lane_is_low((tile, LANES))
    same = (
        lax.broadcasted_iota(jnp.int32, (2 * tile, tile), 0) % tile // members
        == lax.broadcasted_iota(jnp.int32, (2 * tile, tile), 1) // members
    )
    ones = jnp.ones((tile, LANES), jnp.bfloat16)

    def score(rows, lanes):
        queries = qs[rows, lanes]
        none = jnp.zeros_like(queries)
        both = jnp.concatenate(
            [jnp.where(low, queries, none), jnp.where(low, none, queries)], axis=0
        )
        return lax.dot_general(both, ks[rows, lanes], NT, preferred_element_type=jnp.float32)

    work = [
        (slice(g * tile, (g + 1) * tile), lane_slice(pair))
        for g in range(total // tile)
        for pair in range(HEADS // 2)
    ]
    later = score(*work[0])
    for i, (rows, lanes) in enumerate(work):
        scores = jnp.where(same, later, -jnp.inf)
        if i + 1 < len(work):
            later = score(*work[i + 1])
        peaks = jnp.max(scores, axis=-1, keepdims=True)
        weights = jnp.exp2(scores - peaks).astype(jnp.bfloat16)
        mixed = dot(weights, jnp.concatenate([vs[rows, lanes], ones], axis=1))
        done = mixed[:, :LANES] / mixed[:, LANES:]
        att[rows, lanes] = jnp.where(low, done[:tile], done[tile:]).astype(jnp.bfloat16)

    for b in range(total // mlp_block):
        here = slice(b * mlp_block, (b + 1) * mlp_block)
        share = mlp_block // block
        x = jnp.concatenate(xs[b * share : (b + 1) * share], axis=0)
        after = (x + dot(att[here, :], wout_ref[...])).astype(jnp.bfloat16).astype(jnp.float32)
        out = after
        n = normed(after, gain2_ref[...])
        up = dot(n, wup_ref[:, :ff_step])
        for j in range(0, ff, ff_step):
            later = dot(n, wup_ref[:, j + ff_step : j + 2 * ff_step]) if j + ff_step < ff else None
            hidden = gelu(up).astype(jnp.bfloat16)
            out = out + dot(hidden, wdown_ref[j : j + ff_step, :])
            up = later
        for t in range(mlp_block // members):
            token = b * (mlp_block // members) + t
            for c in columns:
                rows32[c, pl.ds(token, members, stride=tokens), :] = out[
                    t * members : (t + 1) * members, lane_slice(c)
                ]
    for c in columns:
        o_ref[:, :, lane_slice(c)] = (
            rows32[c].astype(jnp.bfloat16).reshape(members, tokens, LANES)
        )


def member_part(x, gain, wqkv, wout, gain2, wup, wdown, block=256, mlp_block=1024, ff_step=256):
    members, tokens, width = x.shape
    total, ff = members * tokens, wup.shape[1]
    in_vmem = pl.BlockSpec(memory_space=pltpu.VMEM)
    return pl.pallas_call(
        functools.partial(member_kernel, block, mlp_block, ff_step),
        in_specs=[in_vmem] * 7,
        out_specs=in_vmem,
        out_shape=jax.ShapeDtypeStruct((members, tokens, width), jnp.bfloat16),
        scratch_shapes=[pltpu.VMEM((width // LANES, total, LANES), jnp.float32)]
        + [pltpu.VMEM((total, width), jnp.bfloat16)] * 4,
        compiler_params=params(32),
        cost_estimate=cost(total * width * 2 * (4 * width + 2 * ff) * 2, 6 * total * width),
        name="member_part",
    )(x, gain, wqkv, wout, gain2, wup, wdown)


def per_device(
    state_field,
    gain_space,
    w_qkv_space,
    w_out_space,
    gain_member,
    w_qkv_member,
    w_out_member,
    gain_mlp,
    w_up,
    w_down,
):
    mem_dev, tok_dev, width = state_field.shape
    n_y, n_xl, n_z, n_xh = (lax.axis_size(name) for name in ("y", "xl", "z", "xh"))
    gain_space, gain_member, gain_mlp = (g[None] for g in (gain_space, gain_member, gain_mlp))
    with jax.named_scope("tokens_to_member"):
        mine = lax.all_to_all(state_field, ("xh", "z"), split_axis=0, concat_axis=0, tiled=True)
    x = mine.reshape(n_xh * n_z * tok_dev, width)
    with jax.named_scope("rows_of_other_core"):
        x_other = lax.ppermute(x, "core", [(0, 1), (1, 0)])
    q, kt, v = project_qkv(x, gain_space, w_qkv_space, True)
    kt_other, v_other = project_qkv(x_other, gain_space, w_qkv_space, False)
    order = (n_xh, n_z, n_xl, n_y)
    after_space = attend(q, kt, kt_other, v, v_other, x, w_out_space, order)
    here = tok_dev // (n_y * n_xl)
    sent = after_space.reshape(math.prod(order), here, width)
    with jax.named_scope("members_to_tokens"):
        tokens = lax.all_to_all(
            sent, ("xh", "z", "xl", "y"), split_axis=0, concat_axis=0, tiled=True
        )
    out = member_part(tokens, gain_member, w_qkv_member, w_out_member, gain_mlp, w_up, w_down)
    out = out.reshape(n_xh * n_z, n_xl * n_y, here, width).transpose(1, 0, 2, 3)
    with jax.named_scope("tokens_back"):
        back = lax.all_to_all(out, ("xl", "y"), split_axis=0, concat_axis=0, tiled=True)
    back = back.reshape(n_xl, n_y, n_xh, n_z, here, width).transpose(2, 3, 1, 0, 4, 5)
    return back.reshape(mem_dev, tok_dev, width)


def solution(mesh):
    grid = Mesh(mesh.devices.reshape(4, 2, 4, 2, 2), ("y", "xl", "z", "xh", "core"))
    rows = P(("y", "xl"), ("z", "xh", "core"), None)
    return jax.shard_map(
        per_device, mesh=grid, in_specs=(rows,) + (P(),) * 9, out_specs=rows, check_vma=False
    )
```
